512 devices in a mesh: vertex: 64 (over x, z, core), feat: 8 (over y).
Axes of the slice: x: 4, y: 8, z: 8, core: 2. Of those that a mesh axis runs over, the one named last changes fastest.
Arguments:
- node_feats: bfloat16 [65536, 128], P('vertex', 'feat'), may hold values from -6 to 6
- adj_tiles: bfloat16 [512, 6, 128, 128], P('vertex'), may hold values from 0 to 1
- tile_cols: int32 [512, 6], P('vertex'), may hold values from 0 to 511, as said below
- degrees: int32 [65536], P('vertex'), may hold values from 8 to 64
- w_self: bfloat16 [128, 256], P('feat'), may hold values from -0.375 to 0.375
- w_neigh: bfloat16 [128, 256], P('feat'), may hold values from -0.375 to 0.375
- hidden_bias: float32 [256], replicated, may hold values from -3 to 3
- cotangent: bfloat16 [65536, 256], P(('vertex', 'feat')), may hold values from -6 to 6
Outputs:
- hidden: bfloat16 [65536, 256], P(('vertex', 'feat'))
- grad_self: float32 [128, 256], P('feat')
- grad_neigh: float32 [128, 256], P('feat')
- grad_bias: float32 [256], replicated
The draws below stay inside these ranges and needn't reach their ends.
Inputs may be any that keep to these rules, and one draw needn't show every extreme that they name: `tile_cols`: row block r lies on vertex index r // 8; each of its tiles' column blocks lies on the same vertex index or on one of the two next to it, cyclically (index 0 next to the last).
All inputs are finite; a program needn't handle non-finite values.
Results may differ from the reference program's by a relative error of at most 0.019.
Values may be sent and summed in bfloat16 or wider, within the bound.
No kernel may reach another device: no remote copies, remote signals or barrier semaphores. Data moves between devices by JAX's collectives and lax.ppermute only.
A program may use at most 64 MiB of HBM per device.

```python
import jax
import jax.numpy as jnp
from jax import lax

F = 128
H = 256
TILE = 128
KT = 6
BLK_DEV = 8
NBLK = 512
NODES = 65536


def draw_tile_cols(key, part):
    key = jax.random.fold_in(key, 7)
    owner = jnp.arange(NBLK, dtype=jnp.int32) // BLK_DEV
    offset = jax.random.randint(key, (NBLK, KT), -BLK_DEV, 2 * BLK_DEV, dtype=jnp.int32)
    return (owner[:, None] * BLK_DEV + offset) % NBLK


def touch_ends(entries, key, smallest, high):
    longest = entries.shape.index(max(entries.shape))
    spots = []
    for shift in (0, 1):
        where = [jax.random.randint(jax.random.fold_in(key, axis), (), 0, length) for axis, length in enumerate(entries.shape)]
        where[longest] = (where[longest] + shift) % entries.shape[longest]
        spots.append(tuple(where))
    return entries.at[spots[0]].set(smallest).at[spots[1]].set(high)


def block_levels(stream_key, shape, split, low, top_value):
    level = 1.0
    for position, parts in split:
        draws = jax.random.uniform(jax.random.fold_in(jax.random.fold_in(stream_key, 6), position), (parts,), jnp.float32, low / len(split), top_value / len(split))
        level = level * jnp.repeat(jnp.exp(draws), shape[position] // parts).reshape((-1,) + (1,) * (len(shape) - 1 - position))
    return level


def normal_values(stream_key, dims, width, bound, pieces=(), kind=jnp.bfloat16):
    gain = block_levels(stream_key, dims, pieces, -0.22, 0.18) if pieces else 1.0
    array = jax.random.normal(stream_key, dims, jnp.float32) * width * gain
    return jnp.minimum(jnp.maximum(array, -bound), bound).astype(kind)


def setup_inputs(seed: int = 0) -> dict:
    seeds = jax.random.split(jax.random.key(seed), 9)
    return {
        "node_feats": normal_values(seeds[0], (NODES, F), 1.0, 6.0, ((0, 64), (1, 8))),
        "adj_tiles": jnp.clip(1.0 * jax.random.uniform(seeds[1], (NBLK, KT, TILE, TILE), jnp.float32) ** block_levels(seeds[1], (NBLK, KT, TILE, TILE), ((0, 64),), -0.2, 0.2), 0.0, 1.0).astype(jnp.bfloat16),
        "tile_cols": draw_tile_cols(jax.random.fold_in(seeds[8], 71), 0),
        "degrees": touch_ends(jax.random.randint(seeds[3], (NODES,), 8, 65), jax.random.fold_in(seeds[3], 1), 8, 64).astype(jnp.int32),
        "w_self": normal_values(seeds[4], (F, H), (2 * F) ** -0.5, 0.375, ((0, 8),)),
        "w_neigh": normal_values(seeds[5], (F, H), (2 * F) ** -0.5, 0.375, ((0, 8),)),
        "hidden_bias": normal_values(seeds[6], (H,), 0.5, 3.0, (), jnp.float32),
        "cotangent": normal_values(seeds[7], (NODES, H), 1.0, 6.0, ((0, 512),)),
    }


def reference(node_feats, adj_tiles, tile_cols, degrees, w_self, w_neigh, hidden_bias, cotangent):
    blocks = node_feats.reshape(NBLK, TILE, F)

    def one_block(pair):
        tiles_here, cols_here = pair
        picked = blocks[cols_here]
        return jnp.einsum('kij,kjf->if', tiles_here.astype(jnp.float32), picked.astype(jnp.float32))

    summed = lax.map(one_block, (adj_tiles, tile_cols)).reshape(NODES, F)
    averaged = (summed / degrees.astype(jnp.float32)[:, None]).astype(jnp.bfloat16)
    preact = jnp.dot(node_feats, w_self, preferred_element_type=jnp.float32) + jnp.dot(averaged, w_neigh, preferred_element_type=jnp.float32) + hidden_bias
    hidden = jnp.maximum(preact, 0.0).astype(jnp.bfloat16)
    grad_pre = jnp.where(preact > 0, cotangent, jnp.zeros_like(cotangent))
    grad_self = jnp.dot(node_feats.T, grad_pre, preferred_element_type=jnp.float32)
    grad_neigh = jnp.dot(averaged.T, grad_pre, preferred_element_type=jnp.float32)
    grad_bias = jnp.sum(grad_pre.astype(jnp.float32), axis=0)
    return (hidden, grad_self, grad_neigh, grad_bias)
```

```python
import jax
import jax.numpy as jnp
from jax import lax
from jax.sharding import Mesh, PartitionSpec as P

F32 = jnp.float32
BF16 = jnp.bfloat16
VERTEX = ("x", "z", "c")


def shards(node_feats, adj_tiles, tile_cols, degrees, w_self, w_neigh, hidden_bias, cotangent):
    node_count, feat_local = node_feats.shape
    blk_here, _, tile_size, _ = adj_tiles.shape
    vertex_count = lax.axis_size(VERTEX)
    feat_count = lax.axis_size("feat")
    rows_own = node_count // feat_count
    hidden_units = w_self.shape[1]

    forward = [(i, (i + 1) % vertex_count) for i in range(vertex_count)]
    backward = [(target, source) for source, target in forward]
    low = lax.ppermute(node_feats, VERTEX, forward)
    high = lax.ppermute(node_feats, VERTEX, backward)
    blocks = jnp.concatenate([low, node_feats, high], axis=0)
    blocks = blocks.reshape(3 * blk_here, tile_size, feat_local)
    vertex_idx = lax.axis_index(VERTEX)
    local_cols = (tile_cols - vertex_idx * blk_here + blk_here) % (blk_here * vertex_count)
    picked = blocks[local_cols]
    summed = jnp.einsum("bkij,bkjf->bif", adj_tiles, picked, preferred_element_type=F32)
    summed = summed.reshape(node_count, feat_local)
    averaged = (summed / degrees.astype(F32)[:, None]).astype(BF16)

    rows = jnp.concatenate([node_feats, averaged], axis=1).T
    rows = rows.reshape(2 * feat_local, feat_count, rows_own).transpose(1, 0, 2)
    weights = jnp.concatenate([w_self, w_neigh], axis=0)
    half = hidden_units // 2
    weights = jnp.concatenate([weights[:, :half], weights[:, half:]], axis=0)
    packed = jnp.concatenate(
        [rows, jnp.broadcast_to(weights[None], (feat_count,) + weights.shape)], axis=1
    )
    packed = lax.all_to_all(packed, "feat", 0, 0, tiled=True)
    width = 2 * feat_local
    inputs = packed[:, :width].reshape(feat_count * width, rows_own)
    weights = jnp.concatenate([packed[:, width : 2 * width], packed[:, 2 * width :]], axis=2)
    weights = weights.reshape(feat_count * width, hidden_units)

    preact = (
        lax.dot_general(inputs, weights, (((0,), (0,)), ((), ())), preferred_element_type=F32)
        + hidden_bias
    )
    hidden = jnp.maximum(preact, 0.0).astype(BF16)
    grad_pre = jnp.where(preact > 0, cotangent, jnp.zeros_like(cotangent))
    grads = jnp.dot(inputs, grad_pre, preferred_element_type=F32)
    grads = grads.reshape(feat_count, width, hidden_units)
    bias_row = jnp.sum(grad_pre.astype(F32), axis=0)
    bias_row = jnp.broadcast_to(bias_row, (feat_count, 8, hidden_units))
    grads = jnp.concatenate([grads, bias_row], axis=1)

    grads = lax.all_to_all(grads, "feat", 0, 0, tiled=True).sum(0)
    grads = lax.all_gather(grads, ("x", "c")).sum(0)
    grads = lax.all_gather(grads, "z").sum(0)
    return (hidden, grads[:feat_local], grads[feat_local:width], grads[width])


def solution(mesh):
    sizes = {"x": 4, "z": 8, "c": 2, "feat": 8}
    grid = Mesh(mesh.devices.reshape(tuple(sizes.values())), tuple(sizes))
    return jax.shard_map(
        shards,
        mesh=grid,
        in_specs=(
            P(VERTEX, "feat"),
            P(VERTEX, None, None, None),
            P(VERTEX, None),
            P(VERTEX),
            P("feat", None),
            P("feat", None),
            P(),
            P((*VERTEX, "feat"), None),
        ),
        out_specs=(P((*VERTEX, "feat"), None), P("feat", None), P("feat", None), P()),
        check_vma=False,
    )
```

```python
import functools

import jax
import jax.numpy as jnp
from jax import lax
from jax.experimental import pallas as pl
from jax.experimental.pallas import tpu as pltpu
from jax.sharding import Mesh, PartitionSpec as P

F32 = jnp.float32
BF16 = jnp.bfloat16
VERTEX = ("x", "z", "c")
NT = (((1,), (1,)), ((), ()))
TN = (((0,), (0,)), ((), ()))
VMEM = pl.BlockSpec(memory_space=pltpu.VMEM)
SMEM = pl.BlockSpec(memory_space=pltpu.SMEM)


def call(kernel, out_shape, in_specs, scratch_shapes=(), flops=0):
    many = isinstance(out_shape, (tuple, list))
    return pl.pallas_call(
        kernel,
        out_shape=out_shape,
        in_specs=in_specs,
        out_specs=[VMEM] * len(out_shape) if many else VMEM,
        scratch_shapes=list(scratch_shapes),
        compiler_params=pltpu.CompilerParams(vmem_limit_bytes=32 * 1024 * 1024),
        cost_estimate=pl.CostEstimate(flops=flops, bytes_accessed=2000000, transcendentals=0),
    )


def aggregate_kernel(
    total_blocks, cols_ref, place_ref, pair_ref, far_ref, own_ref, adj_ref, deg_ref, ws_ref, wn_ref, out_ref, feats
):
    blocks, tiles, _, size = adj_ref.shape
    width = own_ref.shape[0]
    half = ws_ref.shape[1] // 2
    for b in range(blocks):
        feats[b] = pair_ref[0, :, b * size : (b + 1) * size]
        feats[blocks + b] = pair_ref[1, :, b * size : (b + 1) * size]
        feats[2 * blocks + b] = far_ref[:, b * size : (b + 1) * size]
    first = place_ref[0]
    turn = place_ref[1]
    for r in range(blocks):
        total = jnp.zeros((width, size), F32)
        for k in range(tiles):
            col = lax.rem(cols_ref[r, k] - first + blocks + total_blocks, total_blocks)
            spot = lax.rem(col + turn, 3 * blocks)
            total += lax.dot_general(feats[spot], adj_ref[r, k], NT, preferred_element_type=F32)
        degree = deg_ref[:, r * size : (r + 1) * size].astype(F32)
        out_ref[r, :width] = own_ref[:, r * size : (r + 1) * size]
        out_ref[r, width : 2 * width] = (total / degree).astype(BF16)
        for h in range(2):
            at = 2 * width * (1 + h)
            out_ref[r, at : at + width] = ws_ref[:, h * half : (h + 1) * half]
            out_ref[r, at + width : at + 2 * width] = wn_ref[:, h * half : (h + 1) * half]


def layer_kernel(width, packed_ref, cot_ref, bias_ref, hidden_ref, grads_ref):
    feat_count = packed_ref.shape[0]
    rows = packed_ref.shape[2]
    half = rows
    inputs = packed_ref[:, : 2 * width].reshape(feat_count * 2 * width, rows)
    left = packed_ref[:, 2 * width : 4 * width].reshape(feat_count * 2 * width, half)
    right = packed_ref[:, 4 * width : 6 * width].reshape(feat_count * 2 * width, half)
    ones = jnp.ones((16, rows), BF16)
    for h, weights in enumerate((left, right)):
        lanes = slice(h * half, (h + 1) * half)
        preact = lax.dot_general(inputs, weights, TN, preferred_element_type=F32) + bias_ref[:, lanes]
        hidden_ref[:, lanes] = jnp.maximum(preact, 0.0).astype(BF16)
        cot = cot_ref[:, lanes].astype(F32)
        grad_pre = jnp.where(preact > 0, cot, 0.0).astype(BF16)
        grads = jnp.dot(inputs, grad_pre, preferred_element_type=F32)
        grads = grads.reshape(feat_count, 2, width, half)
        bias = jnp.dot(ones, grad_pre, preferred_element_type=F32).astype(grads_ref.dtype)
        for c in range(2):
            for f in range(feat_count):
                grads_ref[c, f, h * width : (h + 1) * width] = grads[f, c].astype(grads_ref.dtype)
                if c == h:
                    grads_ref[c, f, 2 * width :] = bias


def sum_kernel(rows_ref, out_ref):
    total = rows_ref[0].astype(F32)
    for i in range(1, rows_ref.shape[0]):
        total += rows_ref[i].astype(F32)
    if len(out_ref.shape) == 2:
        out_ref[...] = total.astype(out_ref.dtype)
    else:
        total = total.astype(out_ref.dtype)
        for i in range(out_ref.shape[0]):
            out_ref[i] = total


def unpack_kernel(width, pair_ref, self_ref, neigh_ref, bias_ref):
    half = pair_ref.shape[2]
    for h in range(2):
        lanes = slice(h * half, (h + 1) * half)
        self_ref[:, lanes] = pair_ref[0, h * width : (h + 1) * width]
        neigh_ref[:, lanes] = pair_ref[1, h * width : (h + 1) * width]
        bias_ref[:, lanes] = pair_ref[h, 2 * width : 2 * width + 1]


def shards(node_feats, adj_tiles, tile_cols, degrees, w_self, w_neigh, hidden_bias, cotangent):
    node_count, width = node_feats.shape
    blocks, tiles, size, _ = adj_tiles.shape
    vertex_count = lax.axis_size(VERTEX)
    feat_count = lax.axis_size("feat")
    chip_count = vertex_count // 2
    rows_own = node_count // feat_count
    hidden_units = w_self.shape[1]

    feats = node_feats.T
    away = [(v, (v - 1 if v % 2 == 0 else v + 1) % vertex_count) for v in range(vertex_count)]
    far = lax.ppermute(feats, VERTEX, away)
    pair = lax.all_gather(feats, "c")
    vertex_idx = lax.axis_index(VERTEX)
    core = lax.axis_index("c")
    place = jnp.stack([vertex_idx * blocks, (1 - core) * (2 * blocks)]).astype(jnp.int32)
    packed = call(
        functools.partial(aggregate_kernel, blocks * vertex_count),
        jax.ShapeDtypeStruct((feat_count, 6 * width, rows_own), BF16),
        [SMEM, SMEM] + [VMEM] * 7,
        [pltpu.VMEM((3 * blocks, width, size), BF16)],
        flops=2 * blocks * tiles * size * size * width,
    )(tile_cols, place, pair, far, feats, adj_tiles, degrees.reshape(1, -1), w_self, w_neigh)

    packed = lax.all_to_all(packed, "feat", 0, 0, tiled=True)
    hidden, grads = call(
        functools.partial(layer_kernel, width),
        (
            jax.ShapeDtypeStruct((rows_own, hidden_units), BF16),
            jax.ShapeDtypeStruct((2, feat_count, 3 * width, rows_own), BF16),
        ),
        [VMEM] * 3,
        flops=4 * rows_own * 256 * hidden_units,
    )(packed, cotangent, hidden_bias.reshape(1, -1))

    grads = lax.all_to_all(
        grads.reshape(2 * feat_count, 3 * width, rows_own), ("c", "feat"), 0, 0, tiled=True
    )
    grads = call(
        sum_kernel, jax.ShapeDtypeStruct((chip_count, 3 * width, rows_own), BF16), [VMEM]
    )(grads)
    grads = lax.all_to_all(grads, ("x", "z"), 0, 0, tiled=True)
    grads = call(sum_kernel, jax.ShapeDtypeStruct((3 * width, rows_own), F32), [VMEM])(grads)
    pair = lax.all_gather(grads, "c")
    grad_self, grad_neigh, grad_bias = call(
        functools.partial(unpack_kernel, width),
        (
            jax.ShapeDtypeStruct((width, hidden_units), F32),
            jax.ShapeDtypeStruct((width, hidden_units), F32),
            jax.ShapeDtypeStruct((1, hidden_units), F32),
        ),
        [VMEM],
    )(pair)
    return (hidden, grad_self, grad_neigh, grad_bias.reshape(hidden_units))


def solution(mesh):
    sizes = {"x": 4, "z": 8, "c": 2, "feat": 8}
    grid = Mesh(mesh.devices.reshape(tuple(sizes.values())), tuple(sizes))
    return jax.shard_map(
        shards,
        mesh=grid,
        in_specs=(
            P(VERTEX, "feat"),
            P(VERTEX, None, None, None),
            P(VERTEX, None),
            P(VERTEX),
            P("feat", None),
            P("feat", None),
            P(),
            P((*VERTEX, "feat"), None),
        ),
        out_specs=(P((*VERTEX, "feat"), None), P("feat", None), P("feat", None), P()),
        check_vma=False,
    )
```

```python
import functools

import jax
import jax.numpy as jnp
from jax import lax
from jax.experimental import pallas as pl
from jax.experimental.pallas import tpu as pltpu
from jax.sharding import Mesh, PartitionSpec as P

F32 = jnp.float32
BF16 = jnp.bfloat16
VERTEX = ("x", "z", "c")
NT = (((1,), (1,)), ((), ()))
TN = (((0,), (0,)), ((), ()))
VMEM = pl.BlockSpec(memory_space=pltpu.VMEM)
SMEM = pl.BlockSpec(memory_space=pltpu.SMEM)


def call(kernel, out_shape, in_specs, scratch_shapes=(), flops=0, out_specs=None):
    if out_specs is None:
        out_specs = [VMEM] * len(out_shape) if isinstance(out_shape, tuple) else VMEM
    return pl.pallas_call(
        kernel,
        out_shape=out_shape,
        in_specs=in_specs,
        out_specs=out_specs,
        scratch_shapes=list(scratch_shapes),
        compiler_params=pltpu.CompilerParams(vmem_limit_bytes=32 * 1024 * 1024),
        cost_estimate=pl.CostEstimate(flops=flops, bytes_accessed=2000000, transcendentals=0),
    )


def places_kernel(total_blocks, cols_ref, place_ref, spots_ref):
    blocks, tiles = cols_ref.shape
    first = place_ref[0]
    turn = place_ref[1]
    for r in range(blocks):
        for k in range(tiles):
            col = cols_ref[r, k] - first + blocks
            col = jnp.where(col < 0, col + total_blocks, col)
            col = jnp.where(col >= total_blocks, col - total_blocks, col)
            spot = col + turn
            spots_ref[r, k] = jnp.where(spot >= 3 * blocks, spot - 3 * blocks, spot)


def aggregate_kernel(spots_ref, pair_ref, far_ref, own_ref, adj_ref, deg_ref, ws_ref, wn_ref, out_ref, feats):
    blocks, tiles, _, size = adj_ref.shape
    width = own_ref.shape[0]
    half = ws_ref.shape[1] // 2
    for b in range(blocks):
        feats[b] = pair_ref[0, :, b * size : (b + 1) * size]
        feats[blocks + b] = pair_ref[1, :, b * size : (b + 1) * size]
        feats[2 * blocks + b] = far_ref[:, b * size : (b + 1) * size]
    for r in range(blocks):
        picked = jnp.concatenate([feats[spots_ref[r, k]] for k in range(tiles)], axis=1)
        weights = jnp.concatenate([adj_ref[r, k] for k in range(tiles)], axis=1)
        total = lax.dot_general(picked, weights, NT, preferred_element_type=F32)
        degree = deg_ref[:, r * size : (r + 1) * size].astype(F32)
        out_ref[r, :width] = own_ref[:, r * size : (r + 1) * size]
        out_ref[r, width : 2 * width] = (total / degree).astype(BF16)
        for h in range(2):
            at = 2 * width * (1 + h)
            out_ref[r, at : at + width] = ws_ref[:, h * half : (h + 1) * half]
            out_ref[r, at + width : at + 2 * width] = wn_ref[:, h * half : (h + 1) * half]


def layer_kernel(width, packed_ref, cot_ref, bias_ref, hidden_ref, grads_ref):
    feat_count = packed_ref.shape[0]
    rows = packed_ref.shape[2]
    half = rows
    inputs = packed_ref[:, : 2 * width].reshape(feat_count * 2 * width, rows)
    left = packed_ref[:, 2 * width : 4 * width].reshape(feat_count * 2 * width, half)
    right = packed_ref[:, 4 * width : 6 * width].reshape(feat_count * 2 * width, half)
    ones = jnp.ones((8, rows), BF16)
    for h, weights in enumerate((left, right)):
        lanes = slice(h * half, (h + 1) * half)
        preact = lax.dot_general(inputs, weights, TN, preferred_element_type=F32) + bias_ref[:, lanes]
        hidden_ref[:, lanes] = jnp.maximum(preact, 0.0).astype(BF16)
        cot = cot_ref[:, lanes].astype(F32)
        grad_pre = jnp.where(preact > 0, cot, 0.0).astype(BF16)
        grads = jnp.dot(inputs, grad_pre, preferred_element_type=F32)
        grads = grads.reshape(feat_count, 2, width, half)
        bias = jnp.dot(ones, grad_pre, preferred_element_type=F32).astype(grads_ref.dtype)
        for c in range(2):
            for f in range(feat_count):
                grads_ref[c, f, h * width : (h + 1) * width] = grads[f, c].astype(grads_ref.dtype)
                if c == h:
                    grads_ref[c, f, 2 * width :] = bias


def sum_kernel(rows_ref, out_ref):
    total = rows_ref[0].astype(F32)
    for i in range(1, rows_ref.shape[0]):
        total += rows_ref[i].astype(F32)
    if len(out_ref.shape) == 2:
        out_ref[...] = total.astype(out_ref.dtype)
    else:
        total = total.astype(out_ref.dtype)
        for i in range(out_ref.shape[0]):
            out_ref[i] = total


def unpack_kernel(width, pair_ref, layer_ref, hidden_ref, self_ref, neigh_ref, bias_ref):
    hidden_ref[...] = layer_ref[...]
    half = pair_ref.shape[2]
    for h in range(2):
        lanes = slice(h * half, (h + 1) * half)
        self_ref[:, lanes] = pair_ref[0, h * width : (h + 1) * width]
        neigh_ref[:, lanes] = pair_ref[1, h * width : (h + 1) * width]
        bias_ref[:, lanes] = pair_ref[h, 2 * width : 2 * width + 1]


def shards(node_feats, adj_tiles, tile_cols, degrees, w_self, w_neigh, hidden_bias, cotangent):
    node_count, width = node_feats.shape
    blocks, tiles, size, _ = adj_tiles.shape
    vertex_count = lax.axis_size(VERTEX)
    feat_count = lax.axis_size("feat")
    chip_count = vertex_count // 2
    rows_own = node_count // feat_count
    hidden_units = w_self.shape[1]

    feats = node_feats.T
    away = [(v, (v - 1 if v % 2 == 0 else v + 1) % vertex_count) for v in range(vertex_count)]
    far = lax.ppermute(feats, VERTEX, away)
    pair = lax.all_gather(feats, "c")
    vertex_idx = lax.axis_index(VERTEX)
    core = lax.axis_index("c")
    place = jnp.stack([vertex_idx * blocks, (1 - core) * (2 * blocks)]).astype(jnp.int32)
    spots = call(
        functools.partial(places_kernel, blocks * vertex_count),
        jax.ShapeDtypeStruct((blocks, tiles), jnp.int32),
        [SMEM] * 2,
        flops=5 * 10**9,
        out_specs=SMEM,
    )(tile_cols, place)
    packed = call(
        aggregate_kernel,
        jax.ShapeDtypeStruct((feat_count, 6 * width, rows_own), BF16),
        [SMEM] + [VMEM] * 7,
        [pltpu.VMEM((3 * blocks, width, size), BF16)],
        flops=2 * blocks * tiles * size * size * width,
    )(spots, pair, far, feats, adj_tiles, degrees.reshape(1, -1), w_self, w_neigh)

    packed = lax.all_to_all(packed, "feat", 0, 0, tiled=True)
    hidden, grads = call(
        functools.partial(layer_kernel, width),
        (
            jax.ShapeDtypeStruct((rows_own, hidden_units), BF16),
            jax.ShapeDtypeStruct((2, feat_count, 2 * width + 8, rows_own), BF16),
        ),
        [VMEM] * 3,
        flops=4 * rows_own * 256 * hidden_units,
    )(packed, cotangent, hidden_bias.reshape(1, -1))

    grads = lax.all_to_all(
        grads.reshape(2 * feat_count, 2 * width + 8, rows_own), ("c", "feat"), 0, 0, tiled=True
    )
    grads = call(
        sum_kernel, jax.ShapeDtypeStruct((chip_count, 2 * width + 8, rows_own), BF16), [VMEM]
    )(grads)
    grads = lax.all_to_all(grads, ("x", "z"), 0, 0, tiled=True)
    grads = call(sum_kernel, jax.ShapeDtypeStruct((2 * width + 8, rows_own), F32), [VMEM])(grads)
    pair = lax.all_gather(grads, "c")
    hidden, grad_self, grad_neigh, grad_bias = call(
        functools.partial(unpack_kernel, width),
        (
            jax.ShapeDtypeStruct((rows_own, hidden_units), BF16),
            jax.ShapeDtypeStruct((width, hidden_units), F32),
            jax.ShapeDtypeStruct((width, hidden_units), F32),
            jax.ShapeDtypeStruct((1, hidden_units), F32),
        ),
        [VMEM] * 2,
    )(pair, hidden)
    return (hidden, grad_self, grad_neigh, grad_bias.reshape(hidden_units))


def solution(mesh):
    sizes = {"x": 4, "z": 8, "c": 2, "feat": 8}
    grid = Mesh(mesh.devices.reshape(tuple(sizes.values())), tuple(sizes))
    return jax.shard_map(
        shards,
        mesh=grid,
        in_specs=(
            P(VERTEX, "feat"),
            P(VERTEX, None, None, None),
            P(VERTEX, None),
            P(VERTEX),
            P("feat", None),
            P("feat", None),
            P(),
            P((*VERTEX, "feat"), None),
        ),
        out_specs=(P((*VERTEX, "feat"), None), P("feat", None), P("feat", None), P()),
        check_vma=False,
    )
```

```python
import functools

import jax
import jax.numpy as jnp
from jax import lax
from jax.experimental import pallas as pl
from jax.experimental.pallas import tpu as pltpu
from jax.sharding import Mesh, PartitionSpec as P

F32 = jnp.float32
BF16 = jnp.bfloat16
CHIPS = ("x", "z", "near")
VERTEX = ("x", "z", "near", "c")
NT = (((1,), (1,)), ((), ()))
TN = (((0,), (0,)), ((), ()))
VMEM = pl.BlockSpec(memory_space=pltpu.VMEM)
SMEM = pl.BlockSpec(memory_space=pltpu.SMEM)


def call(kernel, out_shape, in_specs, scratch_shapes=(), flops=0, out_specs=None):
    if out_specs is None:
        out_specs = [VMEM] * len(out_shape) if isinstance(out_shape, tuple) else VMEM
    return pl.pallas_call(
        kernel,
        out_shape=out_shape,
        in_specs=in_specs,
        out_specs=out_specs,
        scratch_shapes=list(scratch_shapes),
        compiler_params=pltpu.CompilerParams(vmem_limit_bytes=32 * 1024 * 1024),
        cost_estimate=pl.CostEstimate(flops=flops, bytes_accessed=2000000, transcendentals=0),
    )


def places_kernel(total_blocks, cols_ref, place_ref, spots_ref):
    blocks, tiles = cols_ref.shape
    first = place_ref[0]
    turn = place_ref[1]
    for r in range(blocks):
        for k in range(tiles):
            col = cols_ref[r, k] - first + blocks
            col = jnp.where(col < 0, col + total_blocks, col)
            col = jnp.where(col >= total_blocks, col - total_blocks, col)
            spot = col + turn
            spots_ref[r, k] = jnp.where(spot >= 3 * blocks, spot - 3 * blocks, spot)


def aggregate_kernel(spots_ref, pair_ref, far_ref, own_ref, adj_ref, deg_ref, ws_ref, wn_ref, out_ref, feats):
    blocks, tiles, _, size = adj_ref.shape
    width = own_ref.shape[0]
    half = ws_ref.shape[1] // 2
    for b in range(blocks):
        feats[b] = pair_ref[0, :, b * size : (b + 1) * size]
        feats[blocks + b] = pair_ref[1, :, b * size : (b + 1) * size]
        feats[2 * blocks + b] = far_ref[:, b * size : (b + 1) * size]
    for r in range(blocks):
        picked = jnp.concatenate([feats[spots_ref[r, k]] for k in range(tiles)], axis=1)
        weights = jnp.concatenate([adj_ref[r, k] for k in range(tiles)], axis=1)
        total = lax.dot_general(picked, weights, NT, preferred_element_type=F32)
        degree = deg_ref[:, r * size : (r + 1) * size].astype(F32)
        out_ref[r, :width] = own_ref[:, r * size : (r + 1) * size]
        out_ref[r, width : 2 * width] = (total / degree).astype(BF16)
        for h in range(2):
            at = 2 * width * (1 + h)
            out_ref[r, at : at + width] = ws_ref[:, h * half : (h + 1) * half]
            out_ref[r, at + width : at + 2 * width] = wn_ref[:, h * half : (h + 1) * half]


def layer_kernel(width, packed_ref, cot_ref, bias_ref, hidden_ref, grads_ref):
    feat_count = packed_ref.shape[0]
    rows = packed_ref.shape[2]
    half = rows
    pairs = width // 4
    inputs = packed_ref[:, : 2 * width].reshape(feat_count * 2 * width, rows)
    left = packed_ref[:, 2 * width : 4 * width].reshape(feat_count * 2 * width, half)
    right = packed_ref[:, 4 * width : 6 * width].reshape(feat_count * 2 * width, half)
    ones = jnp.ones((8, rows), BF16)
    bias = []
    for h, weights in enumerate((left, right)):
        lanes = slice(h * half, (h + 1) * half)
        preact = lax.dot_general(inputs, weights, TN, preferred_element_type=F32) + bias_ref[:, lanes]
        hidden_ref[:, lanes] = jnp.maximum(preact, 0.0).astype(BF16)
        cot = cot_ref[:, lanes].astype(F32)
        grad_pre = jnp.where(preact > 0, cot, 0.0).astype(BF16)
        grads = jnp.dot(inputs, grad_pre, preferred_element_type=F32)
        bias.append(jnp.dot(ones, grad_pre, preferred_element_type=F32)[:1])
        for f in range(feat_count):
            for c in range(2):
                for near in range(2):
                    first = (f * 2 + c) * width + near * 2 * pairs
                    for i in range(pairs):
                        pair = grads[first + 2 * i : first + 2 * i + 2]
                        grads_ref[near, c, f, h * pairs + i] = pair.astype(BF16)
    bias = jnp.concatenate(bias, axis=0).astype(BF16)
    for f in range(feat_count):
        for c in range(2):
            for near in range(2):
                grads_ref[near, c, f, 2 * pairs] = bias


def sum_kernel(rows_ref, out_ref):
    total = rows_ref[0].astype(F32)
    for i in range(1, rows_ref.shape[0]):
        total += rows_ref[i].astype(F32)
    total = total.astype(out_ref.dtype)
    for i in range(out_ref.shape[0]):
        out_ref[i] = total


def total_kernel(rows_ref, grads_ref, bias_ref):
    pairs = (rows_ref.shape[1] - 1) // 2
    half = rows_ref.shape[3]
    for near in range(2):
        total = rows_ref[near].astype(F32)
        for i in range(near + 2, rows_ref.shape[0], 2):
            total += rows_ref[i].astype(F32)
        for h in range(2):
            lanes = slice(h * half, (h + 1) * half)
            for i in range(pairs):
                first = 2 * (near * pairs + i)
                grads_ref[first : first + 2, lanes] = total[h * pairs + i]
            if near == 0:
                bias_ref[:, lanes] = total[2 * pairs, h : h + 1]


def output_kernel(pair_ref, total_ref, layer_ref, hidden_ref, self_ref, neigh_ref, bias_ref):
    hidden_ref[...] = layer_ref[...]
    self_ref[...] = pair_ref[0]
    neigh_ref[...] = pair_ref[1]
    bias_ref[...] = total_ref[...]


def shards(node_feats, adj_tiles, tile_cols, degrees, w_self, w_neigh, hidden_bias, cotangent):
    node_count, width = node_feats.shape
    blocks, tiles, size, _ = adj_tiles.shape
    vertex_count = lax.axis_size(VERTEX)
    feat_count = lax.axis_size("feat")
    chip_count = vertex_count // 2
    rows_own = node_count // feat_count
    hidden_units = w_self.shape[1]

    feats = node_feats.T
    away = [(v, (v - 1 if v % 2 == 0 else v + 1) % vertex_count) for v in range(vertex_count)]
    far = lax.ppermute(feats, VERTEX, away)
    pair = lax.all_gather(feats, "c")
    vertex_idx = lax.axis_index(VERTEX)
    core = lax.axis_index("c")
    place = jnp.stack([vertex_idx * blocks, (1 - core) * (2 * blocks)]).astype(jnp.int32)
    spots = call(
        functools.partial(places_kernel, blocks * vertex_count),
        jax.ShapeDtypeStruct((blocks, tiles), jnp.int32),
        [SMEM] * 2,
        flops=5 * 10**9,
        out_specs=SMEM,
    )(tile_cols, place)
    packed = call(
        aggregate_kernel,
        jax.ShapeDtypeStruct((feat_count, 6 * width, rows_own), BF16),
        [SMEM] + [VMEM] * 7,
        [pltpu.VMEM((3 * blocks, width, size), BF16)],
        flops=2 * blocks * tiles * size * size * width,
    )(spots, pair, far, feats, adj_tiles, degrees.reshape(1, -1), w_self, w_neigh)

    packed = lax.all_to_all(packed, "feat", 0, 0, tiled=True)
    near_count = lax.axis_size("near")
    peers = near_count * 2 * feat_count
    pieces = (width // 2 + 1, 2, rows_own)
    hidden, grads = call(
        functools.partial(layer_kernel, width),
        (
            jax.ShapeDtypeStruct((rows_own, hidden_units), BF16),
            jax.ShapeDtypeStruct((near_count, 2, feat_count, *pieces), BF16),
        ),
        [VMEM] * 3,
        flops=4 * rows_own * 256 * hidden_units,
    )(packed, cotangent, hidden_bias.reshape(1, -1))

    grads = lax.all_to_all(grads.reshape(peers, *pieces), ("near", "c", "feat"), 0, 0, tiled=True)
    grads = call(sum_kernel, jax.ShapeDtypeStruct((chip_count, *pieces), BF16), [VMEM])(grads)
    grads = lax.all_to_all(grads, CHIPS, 0, 0, tiled=True)
    grads, grad_bias = call(
        total_kernel,
        (
            jax.ShapeDtypeStruct((width, hidden_units), F32),
            jax.ShapeDtypeStruct((1, hidden_units), F32),
        ),
        [VMEM],
    )(grads)
    pair = lax.all_gather(grads, "c")
    hidden, grad_self, grad_neigh, grad_bias = call(
        output_kernel,
        (
            jax.ShapeDtypeStruct((rows_own, hidden_units), BF16),
            jax.ShapeDtypeStruct((width, hidden_units), F32),
            jax.ShapeDtypeStruct((width, hidden_units), F32),
            jax.ShapeDtypeStruct((1, hidden_units), F32),
        ),
        [VMEM] * 3,
    )(pair, grad_bias, hidden)
    return (hidden, grad_self, grad_neigh, grad_bias.reshape(hidden_units))


def solution(mesh):
    sizes = {"x": 4, "z": 4, "near": 2, "c": 2, "feat": 8}
    grid = Mesh(mesh.devices.reshape(tuple(sizes.values())), tuple(sizes))
    return jax.shard_map(
        shards,
        mesh=grid,
        in_specs=(
            P(VERTEX, "feat"),
            P(VERTEX, None, None, None),
            P(VERTEX, None),
            P(VERTEX),
            P("feat", None),
            P("feat", None),
            P(),
            P((*VERTEX, "feat"), None),
        ),
        out_specs=(P((*VERTEX, "feat"), None), P("feat", None), P("feat", None), P()),
        check_vma=False,
    )
```

```python
import functools

import jax
import jax.numpy as jnp
from jax import lax
from jax.experimental import pallas as pl
from jax.experimental.pallas import tpu as pltpu
from jax.sharding import Mesh, PartitionSpec as P

F32 = jnp.float32
BF16 = jnp.bfloat16
CHIPS = ("x", "z", "near")
VERTEX = ("x", "z", "near", "c")
NT = (((1,), (1,)), ((), ()))
TN = (((0,), (0,)), ((), ()))
VMEM = pl.BlockSpec(memory_space=pltpu.VMEM)
SMEM = pl.BlockSpec(memory_space=pltpu.SMEM)


def call(kernel, out_shape, in_specs, scratch_shapes=(), flops=0, out_specs=None):
    if out_specs is None:
        out_specs = [VMEM] * len(out_shape) if isinstance(out_shape, tuple) else VMEM
    return pl.pallas_call(
        kernel,
        out_shape=out_shape,
        in_specs=in_specs,
        out_specs=out_specs,
        scratch_shapes=list(scratch_shapes),
        compiler_params=pltpu.CompilerParams(vmem_limit_bytes=32 * 1024 * 1024),
        cost_estimate=pl.CostEstimate(flops=flops, bytes_accessed=2000000, transcendentals=0),
    )


def place_kernel(blocks, where_ref, place_ref):
    place_ref[...] = where_ref[...] * blocks


def aggregate_kernel(total_blocks, cols_ref, place_ref, pair_ref, far_ref, adj_ref, deg_ref, ws_ref, wn_ref, out_ref, feats):
    blocks, tiles, _, size = adj_ref.shape
    width = far_ref.shape[0]
    half = ws_ref.shape[1] // 2
    for b in range(blocks):
        feats[b] = pair_ref[0, :, b * size : (b + 1) * size]
        feats[blocks + b] = pair_ref[1, :, b * size : (b + 1) * size]
        feats[2 * blocks + b] = far_ref[:, b * size : (b + 1) * size]
    first = place_ref[0, 0]
    turn = place_ref[1, 0]
    own = place_ref[2, 0]

    def spot(col):
        col = col - first + blocks
        col = jnp.where(col < 0, col + total_blocks, col)
        col = jnp.where(col >= total_blocks, col - total_blocks, col) + turn
        return jnp.where(col >= 3 * blocks, col - 3 * blocks, col)

    for r in range(blocks):
        picked = jnp.concatenate([feats[spot(cols_ref[r, k])] for k in range(tiles)], axis=1)
        weights = jnp.concatenate([adj_ref[r, k] for k in range(tiles)], axis=1)
        total = lax.dot_general(picked, weights, NT, preferred_element_type=F32)
        degree = deg_ref[:, r * size : (r + 1) * size].astype(F32)
        out_ref[r, :width] = feats[own + r]
        out_ref[r, width : 2 * width] = (total / degree).astype(BF16)
        for h in range(2):
            at = 2 * width * (1 + h)
            out_ref[r, at : at + width] = ws_ref[:, h * half : (h + 1) * half]
            out_ref[r, at + width : at + 2 * width] = wn_ref[:, h * half : (h + 1) * half]


def forward_kernel(width, packed_ref, cot_ref, bias_ref, hidden_ref, share_ref):
    feat_count = packed_ref.shape[0]
    rows = packed_ref.shape[2]
    depth = feat_count * 2 * width
    half = rows
    inputs = packed_ref[:, : 2 * width].reshape(depth, rows)
    left = packed_ref[:, 2 * width : 4 * width].reshape(depth, half)
    right = packed_ref[:, 4 * width : 6 * width].reshape(depth, half)
    share_ref[:depth] = inputs
    for h, weights in enumerate((left, right)):
        lanes = slice(h * half, (h + 1) * half)
        preact = lax.dot_general(inputs, weights, TN, preferred_element_type=F32) + bias_ref[:, lanes]
        hidden_ref[:, lanes] = jnp.maximum(preact, 0.0).astype(BF16)
        cot = cot_ref[:, lanes].astype(F32)
        share_ref[depth + h * rows : depth + (h + 1) * rows] = jnp.where(preact > 0, cot, 0.0).astype(BF16)


def backward_kernel(width, pair_ref, place_ref, grads_ref):
    feat_count = grads_ref.shape[1]
    pairs = width // 2
    depth = feat_count * 2 * width
    rows = (pair_ref.shape[1] - depth) // 2
    core = jnp.broadcast_to(place_ref[2:3], (rows, pair_ref.shape[2]))
    inputs = jnp.concatenate([pair_ref[c, :depth] for c in range(2)], axis=1)
    grad_pre = jnp.concatenate(
        [
            jnp.where(
                core == 0,
                pair_ref[c, depth : depth + rows].astype(F32),
                pair_ref[c, depth + rows :].astype(F32),
            ).astype(BF16)
            for c in range(2)
        ],
        axis=0,
    )
    grads = jnp.dot(inputs, grad_pre, preferred_element_type=F32)
    ones = jnp.ones((8, 2 * rows), BF16)
    bias = jnp.dot(ones, grad_pre, preferred_element_type=F32)[:1]
    bias = jnp.concatenate([bias, jnp.zeros_like(bias)], axis=0).astype(BF16)
    for f in range(feat_count):
        for near in range(2):
            for i in range(pairs):
                first = (f * 2 + near) * width + 2 * i
                grads_ref[near, f, i] = grads[first : first + 2].astype(BF16)
            grads_ref[near, f, pairs] = bias


def sum_kernel(rows_ref, out_ref):
    total = rows_ref[0].astype(F32)
    for i in range(1, rows_ref.shape[0]):
        total += rows_ref[i].astype(F32)
    total = total.astype(out_ref.dtype)
    for i in range(out_ref.shape[0]):
        out_ref[i] = total


def total_kernel(rows_ref, out_ref):
    pairs = rows_ref.shape[1] - 1
    for near in range(2):
        total = rows_ref[near].astype(F32)
        for i in range(near + 2, rows_ref.shape[0], 2):
            total += rows_ref[i].astype(F32)
        for i in range(pairs):
            first = 2 * (near * pairs + i)
            out_ref[first : first + 2] = total[i]
        if near == 0:
            out_ref[4 * pairs :] = jnp.zeros((out_ref.shape[0] - 4 * pairs, out_ref.shape[1]), F32)
            out_ref[4 * pairs : 4 * pairs + 2] = total[pairs]


def output_kernel(pair_ref, layer_ref, hidden_ref, self_ref, neigh_ref, bias_ref):
    width = self_ref.shape[0]
    half = pair_ref.shape[2]
    hidden_ref[...] = layer_ref[...]
    for h in range(2):
        lanes = slice(h * half, (h + 1) * half)
        self_ref[:, lanes] = pair_ref[h, :width]
        neigh_ref[:, lanes] = pair_ref[h, width : 2 * width]
        bias_ref[:, lanes] = pair_ref[h, 2 * width : 2 * width + 1]


def shards(node_feats, adj_tiles, tile_cols, degrees, w_self, w_neigh, hidden_bias, cotangent):
    node_count, width = node_feats.shape
    blocks, tiles, size, _ = adj_tiles.shape
    vertex_count = lax.axis_size(VERTEX)
    feat_count = lax.axis_size("feat")
    chip_count = vertex_count // 2
    rows_own = node_count // feat_count
    hidden_units = w_self.shape[1]

    feats = node_feats.T
    away = [(v, (v - 1 if v % 2 == 0 else v + 1) % vertex_count) for v in range(vertex_count)]
    far = lax.ppermute(feats, VERTEX, away)
    pair = lax.all_gather(feats, "c")
    vertex_idx = lax.axis_index(VERTEX)
    core = lax.axis_index("c")
    where = jnp.stack([vertex_idx, 2 * (1 - core), core]).astype(jnp.int32)
    place = call(
        functools.partial(place_kernel, blocks),
        jax.ShapeDtypeStruct((3, size), jnp.int32),
        [VMEM],
        flops=5 * 10**9,
    )(jnp.broadcast_to(where[:, None], (3, size)))
    packed = call(
        functools.partial(aggregate_kernel, blocks * vertex_count),
        jax.ShapeDtypeStruct((feat_count, 6 * width, rows_own), BF16),
        [SMEM] * 2 + [VMEM] * 6,
        [pltpu.VMEM((3 * blocks, width, size), BF16)],
        flops=2 * blocks * tiles * size * size * width,
    )(tile_cols, place, pair, far, adj_tiles, degrees.reshape(1, -1), w_self, w_neigh)

    packed = lax.all_to_all(packed, "feat", 0, 0, tiled=True)
    near_count = lax.axis_size("near")
    depth = feat_count * 2 * width
    pieces = (width // 2 + 1, 2, rows_own)
    hidden, share = call(
        functools.partial(forward_kernel, width),
        (
            jax.ShapeDtypeStruct((rows_own, hidden_units), BF16),
            jax.ShapeDtypeStruct((depth + 2 * rows_own, rows_own), BF16),
        ),
        [VMEM] * 3,
        flops=2 * rows_own * depth * hidden_units,
    )(packed, cotangent, hidden_bias.reshape(1, -1))
    pair = lax.all_gather(share, "c")
    grads = call(
        functools.partial(backward_kernel, width),
        jax.ShapeDtypeStruct((near_count, feat_count, *pieces), BF16),
        [VMEM] * 2,
        flops=2 * rows_own * depth * hidden_units,
    )(pair, place)

    grads = lax.all_to_all(grads.reshape(near_count * feat_count, *pieces), ("near", "feat"), 0, 0, tiled=True)
    grads = call(sum_kernel, jax.ShapeDtypeStruct((chip_count, *pieces), BF16), [VMEM])(grads)
    grads = lax.all_to_all(grads, CHIPS, 0, 0, tiled=True)
    grads = call(total_kernel, jax.ShapeDtypeStruct((2 * width + 8, rows_own), F32), [VMEM])(grads)
    pair = lax.all_gather(grads, "c")
    hidden, grad_self, grad_neigh, grad_bias = call(
        output_kernel,
        (
            jax.ShapeDtypeStruct((rows_own, hidden_units), BF16),
            jax.ShapeDtypeStruct((width, hidden_units), F32),
            jax.ShapeDtypeStruct((width, hidden_units), F32),
            jax.ShapeDtypeStruct((1, hidden_units), F32),
        ),
        [VMEM] * 2,
    )(pair, hidden)
    return (hidden, grad_self, grad_neigh, grad_bias.reshape(hidden_units))


def solution(mesh):
    sizes = {"x": 4, "z": 4, "near": 2, "c": 2, "feat": 8}
    grid = Mesh(mesh.devices.reshape(tuple(sizes.values())), tuple(sizes))
    return jax.shard_map(
        shards,
        mesh=grid,
        in_specs=(
            P(VERTEX, "feat"),
            P(VERTEX, None, None, None),
            P(VERTEX, None),
            P(VERTEX),
            P("feat", None),
            P("feat", None),
            P(),
            P((*VERTEX, "feat"), None),
        ),
        out_specs=(P((*VERTEX, "feat"), None), P("feat", None), P("feat", None), P()),
        check_vma=False,
    )
```

```python
import functools

import jax
import jax.numpy as jnp
from jax import lax
from jax.experimental import pallas as pl
from jax.experimental.pallas import tpu as pltpu
from jax.sharding import Mesh, PartitionSpec as P

F32 = jnp.float32
BF16 = jnp.bfloat16
CHIPS = ("x", "z", "near")
VERTEX = ("x", "z", "near", "c")
NT = (((1,), (1,)), ((), ()))
TN = (((0,), (0,)), ((), ()))
VMEM = pl.BlockSpec(memory_space=pltpu.VMEM)
SMEM = pl.BlockSpec(memory_space=pltpu.SMEM)


def call(kernel, out_shape, in_specs, scratch_shapes=(), flops=0, out_specs=None):
    if out_specs is None:
        out_specs = [VMEM] * len(out_shape) if isinstance(out_shape, tuple) else VMEM
    return pl.pallas_call(
        kernel,
        out_shape=out_shape,
        in_specs=in_specs,
        out_specs=out_specs,
        scratch_shapes=list(scratch_shapes),
        compiler_params=pltpu.CompilerParams(vmem_limit_bytes=32 * 1024 * 1024),
        cost_estimate=pl.CostEstimate(flops=flops, bytes_accessed=2000000, transcendentals=0),
    )


def place_kernel(blocks, where_ref, place_ref):
    place_ref[...] = where_ref[...] * blocks


def aggregate_kernel(total_blocks, cols_ref, place_ref, pair_ref, far_ref, adj_ref, deg_ref, ws_ref, wn_ref, out_ref, feats):
    blocks, tiles, _, size = adj_ref.shape
    width = far_ref.shape[0]
    half = ws_ref.shape[1] // 2
    for b in range(blocks):
        feats[b] = pair_ref[0, :, b * size : (b + 1) * size]
        feats[blocks + b] = pair_ref[1, :, b * size : (b + 1) * size]
        feats[2 * blocks + b] = far_ref[:, b * size : (b + 1) * size]
    first = place_ref[0, 0]
    turn = place_ref[1, 0]
    own = place_ref[2, 0]
    weights_here = [jnp.where(own == 0, ref[:, :half], ref[:, half:]) for ref in (ws_ref, wn_ref)]

    def spot(col):
        col = col - first + blocks
        col = jnp.where(col < 0, col + total_blocks, col)
        col = jnp.where(col >= total_blocks, col - total_blocks, col) + turn
        return jnp.where(col >= 3 * blocks, col - 3 * blocks, col)

    for r in range(blocks):
        picked = jnp.concatenate([feats[spot(cols_ref[r, k])] for k in range(tiles)], axis=1)
        weights = jnp.concatenate([adj_ref[r, k] for k in range(tiles)], axis=1)
        total = lax.dot_general(picked, weights, NT, preferred_element_type=F32)
        degree = deg_ref[:, r * size : (r + 1) * size].astype(F32)
        out_ref[r, :width] = feats[own + r]
        out_ref[r, width : 2 * width] = (total / degree).astype(BF16)
        for i, part in enumerate(weights_here):
            out_ref[r, (2 + i) * width : (3 + i) * width] = part


def share_kernel(packed_ref, cot_ref, share_ref):
    feat_count, depth, rows = packed_ref.shape
    depth = feat_count * depth // 2
    share_ref[:depth] = packed_ref[:, : depth // feat_count].reshape(depth, rows)
    share_ref[depth : 2 * depth] = packed_ref[:, depth // feat_count :].reshape(depth, rows)
    for h in range(2):
        share_ref[2 * depth + h * rows : 2 * depth + (h + 1) * rows] = cot_ref[:, h * rows : (h + 1) * rows]


def layer_kernel(packed_ref, pair_ref, place_ref, bias_ref, hidden_ref, grads_ref):
    _, feat_count, pairs, _, half = grads_ref.shape
    pairs -= 1
    rows = packed_ref.shape[2]
    depth = feat_count * 4 * pairs
    cots = 2 * depth
    core = place_ref[2:3]
    inputs = packed_ref[:, : 4 * pairs].reshape(depth, rows)
    weights = packed_ref[:, 4 * pairs :].reshape(depth, half)
    for h in range(2):
        lanes = slice(h * half, (h + 1) * half)
        preact = lax.dot_general(inputs, pair_ref[h, depth:cots], TN, preferred_element_type=F32) + bias_ref[:, lanes]
        hidden_ref[:, lanes] = jnp.maximum(preact, 0.0).astype(BF16)
    bias = jnp.where(core == 0, bias_ref[:, :half], bias_ref[:, half:])
    core = jnp.broadcast_to(core, (rows, half))
    grad_pre = []
    for c in range(2):
        preact = lax.dot_general(pair_ref[c, :depth], weights, TN, preferred_element_type=F32) + bias
        cot = jnp.where(
            core == 0,
            pair_ref[c, cots : cots + rows].astype(F32),
            pair_ref[c, cots + rows :].astype(F32),
        )
        grad_pre.append(jnp.where(preact > 0, cot, 0.0).astype(BF16))
    grad_pre = jnp.concatenate(grad_pre, axis=0)
    inputs = jnp.concatenate([pair_ref[c, :depth] for c in range(2)], axis=1)
    grads = jnp.dot(inputs, grad_pre, preferred_element_type=F32)
    ones = jnp.ones((8, 2 * rows), BF16)
    bias = jnp.dot(ones, grad_pre, preferred_element_type=F32)[:1]
    bias = jnp.concatenate([bias, jnp.zeros_like(bias)], axis=0).astype(BF16)
    for f in range(feat_count):
        for near in range(2):
            for i in range(pairs):
                first = (f * 2 + near) * 2 * pairs + 2 * i
                grads_ref[near, f, i] = grads[first : first + 2].astype(BF16)
            grads_ref[near, f, pairs] = bias


def sum_kernel(rows_ref, out_ref):
    total = rows_ref[0].astype(F32)
    for i in range(1, rows_ref.shape[0]):
        total += rows_ref[i].astype(F32)
    total = total.astype(out_ref.dtype)
    for i in range(out_ref.shape[0]):
        out_ref[i] = total


def total_kernel(rows_ref, out_ref):
    pairs = rows_ref.shape[1] - 1
    for near in range(2):
        total = rows_ref[near].astype(F32)
        for i in range(near + 2, rows_ref.shape[0], 2):
            total += rows_ref[i].astype(F32)
        for i in range(pairs):
            first = 2 * (near * pairs + i)
            out_ref[first : first + 2] = total[i]
        if near == 0:
            out_ref[4 * pairs :] = jnp.zeros((out_ref.shape[0] - 4 * pairs, out_ref.shape[1]), F32)
            out_ref[4 * pairs : 4 * pairs + 2] = total[pairs]


def output_kernel(pair_ref, layer_ref, hidden_ref, self_ref, neigh_ref, bias_ref):
    width = self_ref.shape[0]
    half = pair_ref.shape[2]
    hidden_ref[...] = layer_ref[...]
    for h in range(2):
        lanes = slice(h * half, (h + 1) * half)
        self_ref[:, lanes] = pair_ref[h, :width]
        neigh_ref[:, lanes] = pair_ref[h, width : 2 * width]
        bias_ref[:, lanes] = pair_ref[h, 2 * width : 2 * width + 1]


def shards(node_feats, adj_tiles, tile_cols, degrees, w_self, w_neigh, hidden_bias, cotangent):
    node_count, width = node_feats.shape
    blocks, tiles, size, _ = adj_tiles.shape
    vertex_count = lax.axis_size(VERTEX)
    feat_count = lax.axis_size("feat")
    chip_count = vertex_count // 2
    rows_own = node_count // feat_count
    hidden_units = w_self.shape[1]

    feats = node_feats.T
    away = [(v, (v - 1 if v % 2 == 0 else v + 1) % vertex_count) for v in range(vertex_count)]
    far = lax.ppermute(feats, VERTEX, away)
    pair = lax.all_gather(feats, "c")
    vertex_idx = lax.axis_index(VERTEX)
    core = lax.axis_index("c")
    where = jnp.stack([vertex_idx, 2 * (1 - core), core]).astype(jnp.int32)
    place = call(
        functools.partial(place_kernel, blocks),
        jax.ShapeDtypeStruct((3, size), jnp.int32),
        [VMEM],
        flops=5 * 10**9,
    )(jnp.broadcast_to(where[:, None], (3, size)))
    packed = call(
        functools.partial(aggregate_kernel, blocks * vertex_count),
        jax.ShapeDtypeStruct((feat_count, 4 * width, rows_own), BF16),
        [SMEM] * 2 + [VMEM] * 6,
        [pltpu.VMEM((3 * blocks, width, size), BF16)],
        flops=2 * blocks * tiles * size * size * width,
    )(tile_cols, place, pair, far, adj_tiles, degrees.reshape(1, -1), w_self, w_neigh)

    packed = lax.all_to_all(packed, "feat", 0, 0, tiled=True)
    near_count = lax.axis_size("near")
    depth = feat_count * 2 * width
    pieces = (width // 2 + 1, 2, rows_own)
    share = call(
        share_kernel,
        jax.ShapeDtypeStruct((2 * depth + 2 * rows_own, rows_own), BF16),
        [VMEM] * 2,
    )(packed, cotangent)
    pair = lax.all_gather(share, "c")
    hidden, grads = call(
        layer_kernel,
        (
            jax.ShapeDtypeStruct((rows_own, hidden_units), BF16),
            jax.ShapeDtypeStruct((near_count, feat_count, *pieces), BF16),
        ),
        [VMEM] * 4,
        flops=6 * rows_own * depth * hidden_units,
    )(packed, pair, place, hidden_bias.reshape(1, -1))

    grads = lax.all_to_all(grads.reshape(near_count * feat_count, *pieces), ("near", "feat"), 0, 0, tiled=True)
    grads = call(sum_kernel, jax.ShapeDtypeStruct((chip_count, *pieces), BF16), [VMEM])(grads)
    grads = lax.all_to_all(grads, CHIPS, 0, 0, tiled=True)
    grads = call(total_kernel, jax.ShapeDtypeStruct((2 * width + 8, rows_own), F32), [VMEM])(grads)
    pair = lax.all_gather(grads, "c")
    hidden, grad_self, grad_neigh, grad_bias = call(
        output_kernel,
        (
            jax.ShapeDtypeStruct((rows_own, hidden_units), BF16),
            jax.ShapeDtypeStruct((width, hidden_units), F32),
            jax.ShapeDtypeStruct((width, hidden_units), F32),
            jax.ShapeDtypeStruct((1, hidden_units), F32),
        ),
        [VMEM] * 2,
    )(pair, hidden)
    return (hidden, grad_self, grad_neigh, grad_bias.reshape(hidden_units))


def solution(mesh):
    sizes = {"x": 4, "z": 4, "near": 2, "c": 2, "feat": 8}
    grid = Mesh(mesh.devices.reshape(tuple(sizes.values())), tuple(sizes))
    return jax.shard_map(
        shards,
        mesh=grid,
        in_specs=(
            P(VERTEX, "feat"),
            P(VERTEX, None, None, None),
            P(VERTEX, None),
            P(VERTEX),
            P("feat", None),
            P("feat", None),
            P(),
            P((*VERTEX, "feat"), None),
        ),
        out_specs=(P((*VERTEX, "feat"), None), P("feat", None), P("feat", None), P()),
        check_vma=False,
    )
```

```python
import functools

import jax
import jax.numpy as jnp
from jax import lax
from jax.experimental import pallas as pl
from jax.experimental.pallas import tpu as pltpu
from jax.sharding import Mesh, PartitionSpec as P

F32 = jnp.float32
BF16 = jnp.bfloat16
CHIPS = ("x", "z", "near")
VERTEX = ("x", "z", "near", "c")
NT = (((1,), (1,)), ((), ()))
TN = (((0,), (0,)), ((), ()))
VMEM = pl.BlockSpec(memory_space=pltpu.VMEM)
SMEM = pl.BlockSpec(memory_space=pltpu.SMEM)


def call(kernel, out_shape, in_specs, scratch_shapes=(), flops=0, out_specs=None):
    if out_specs is None:
        out_specs = [VMEM] * len(out_shape) if isinstance(out_shape, tuple) else VMEM
    return pl.pallas_call(
        kernel,
        out_shape=out_shape,
        in_specs=in_specs,
        out_specs=out_specs,
        scratch_shapes=list(scratch_shapes),
        compiler_params=pltpu.CompilerParams(vmem_limit_bytes=32 * 1024 * 1024),
        cost_estimate=pl.CostEstimate(flops=flops, bytes_accessed=2000000, transcendentals=0),
    )


def place_kernel(blocks, where_ref, place_ref):
    place_ref[...] = where_ref[...] * blocks


def aggregate_kernel(total_blocks, cols_ref, place_ref, pair_ref, far_ref, adj_ref, deg_ref, ws_ref, wn_ref, out_ref, feats):
    blocks, tiles, _, size = adj_ref.shape
    width = far_ref.shape[0]
    half = ws_ref.shape[1] // 2
    for b in range(blocks):
        feats[b] = pair_ref[0, :, b * size : (b + 1) * size]
        feats[blocks + b] = pair_ref[1, :, b * size : (b + 1) * size]
        feats[2 * blocks + b] = far_ref[:, b * size : (b + 1) * size]
    first = place_ref[0, 0]
    turn = place_ref[1, 0]
    own = place_ref[2, 0]
    weights_here = [jnp.where(own == 0, ref[:, :half], ref[:, half:]) for ref in (ws_ref, wn_ref)]

    def spot(col):
        col = col - first + blocks
        col = jnp.where(col < 0, col + total_blocks, col)
        col = jnp.where(col >= total_blocks, col - total_blocks, col) + turn
        return jnp.where(col >= 3 * blocks, col - 3 * blocks, col)

    for r in range(blocks):
        picked = jnp.concatenate([feats[spot(cols_ref[r, k])] for k in range(tiles)], axis=1)
        weights = jnp.concatenate([adj_ref[r, k] for k in range(tiles)], axis=1)
        total = lax.dot_general(picked, weights, NT, preferred_element_type=F32)
        degree = deg_ref[:, r * size : (r + 1) * size].astype(F32)
        out_ref[r, :width] = feats[own + r]
        out_ref[r, width : 2 * width] = (total / degree).astype(BF16)
        for i, part in enumerate(weights_here):
            out_ref[r, (2 + i) * width : (3 + i) * width] = part


def share_kernel(packed_ref, cot_ref, share_ref):
    feat_count, depth, rows = packed_ref.shape
    depth = feat_count * depth // 2
    share_ref[:depth] = packed_ref[:, : depth // feat_count].reshape(depth, rows)
    share_ref[depth : 2 * depth] = packed_ref[:, depth // feat_count :].reshape(depth, rows)
    for h in range(2):
        share_ref[2 * depth + h * rows : 2 * depth + (h + 1) * rows] = cot_ref[:, h * rows : (h + 1) * rows]


def layer_kernel(packed_ref, pair_ref, place_ref, bias_ref, hidden_ref, grads_ref):
    _, feat_count, pairs, _, half = grads_ref.shape
    pairs -= 1
    rows = packed_ref.shape[2]
    depth = feat_count * 4 * pairs
    cots = 2 * depth
    core = place_ref[2:3]
    inputs = packed_ref[:, : 4 * pairs].reshape(depth, rows)
    weights = packed_ref[:, 4 * pairs :].reshape(depth, half)
    units = jnp.concatenate([pair_ref[h, depth:cots] for h in range(2)], axis=1)
    preact = lax.dot_general(inputs, units, TN, preferred_element_type=F32) + bias_ref[...]
    hidden_ref[...] = jnp.maximum(preact, 0.0).astype(BF16)
    bias = jnp.where(core == 0, bias_ref[:, :half], bias_ref[:, half:])
    core = jnp.broadcast_to(core, (rows, half))
    inputs = jnp.concatenate([pair_ref[c, :depth] for c in range(2)], axis=1)
    preact = lax.dot_general(inputs, weights, TN, preferred_element_type=F32) + bias
    grad_pre = []
    for c in range(2):
        cot = jnp.where(
            core == 0,
            pair_ref[c, cots : cots + rows].astype(F32),
            pair_ref[c, cots + rows :].astype(F32),
        )
        grad_pre.append(jnp.where(preact[c * rows : (c + 1) * rows] > 0, cot, 0.0).astype(BF16))
    grad_pre = jnp.concatenate(grad_pre, axis=0)
    grads = jnp.dot(inputs, grad_pre, preferred_element_type=F32)
    ones = jnp.ones((8, 2 * rows), BF16)
    bias = jnp.dot(ones, grad_pre, preferred_element_type=F32)[:1]
    bias = jnp.concatenate([bias, jnp.zeros_like(bias)], axis=0).astype(BF16)
    for f in range(feat_count):
        for near in range(2):
            for i in range(pairs):
                first = (f * 2 + near) * 2 * pairs + 2 * i
                grads_ref[near, f, i] = grads[first : first + 2].astype(BF16)
            grads_ref[near, f, pairs] = bias


def sum_kernel(rows_ref, out_ref):
    total = rows_ref[0].astype(F32)
    for i in range(1, rows_ref.shape[0]):
        total += rows_ref[i].astype(F32)
    total = total.astype(out_ref.dtype)
    for i in range(out_ref.shape[0]):
        out_ref[i] = total


def total_kernel(rows_ref, out_ref):
    pairs = rows_ref.shape[1] - 1
    for near in range(2):
        total = rows_ref[near].astype(F32)
        for i in range(near + 2, rows_ref.shape[0], 2):
            total += rows_ref[i].astype(F32)
        for i in range(pairs):
            first = 2 * (near * pairs + i)
            out_ref[first : first + 2] = total[i]
        if near == 0:
            out_ref[4 * pairs :] = jnp.zeros((out_ref.shape[0] - 4 * pairs, out_ref.shape[1]), F32)
            out_ref[4 * pairs : 4 * pairs + 2] = total[pairs]


def output_kernel(pair_ref, layer_ref, hidden_ref, self_ref, neigh_ref, bias_ref):
    width = self_ref.shape[0]
    half = pair_ref.shape[2]
    hidden_ref[...] = layer_ref[...]
    for h in range(2):
        lanes = slice(h * half, (h + 1) * half)
        self_ref[:, lanes] = pair_ref[h, :width]
        neigh_ref[:, lanes] = pair_ref[h, width : 2 * width]
        bias_ref[:, lanes] = pair_ref[h, 2 * width : 2 * width + 1]


def shards(node_feats, adj_tiles, tile_cols, degrees, w_self, w_neigh, hidden_bias, cotangent):
    node_count, width = node_feats.shape
    blocks, tiles, size, _ = adj_tiles.shape
    vertex_count = lax.axis_size(VERTEX)
    feat_count = lax.axis_size("feat")
    chip_count = vertex_count // 2
    rows_own = node_count // feat_count
    hidden_units = w_self.shape[1]

    feats = node_feats.T
    away = [(v, (v - 1 if v % 2 == 0 else v + 1) % vertex_count) for v in range(vertex_count)]
    far = lax.ppermute(feats, VERTEX, away)
    pair = lax.all_gather(feats, "c")
    vertex_idx = lax.axis_index(VERTEX)
    core = lax.axis_index("c")
    where = jnp.stack([vertex_idx, 2 * (1 - core), core]).astype(jnp.int32)
    place = call(
        functools.partial(place_kernel, blocks),
        jax.ShapeDtypeStruct((3, size), jnp.int32),
        [VMEM],
        flops=5 * 10**9,
    )(jnp.broadcast_to(where[:, None], (3, size)))
    packed = call(
        functools.partial(aggregate_kernel, blocks * vertex_count),
        jax.ShapeDtypeStruct((feat_count, 4 * width, rows_own), BF16),
        [SMEM] * 2 + [VMEM] * 6,
        [pltpu.VMEM((3 * blocks, width, size), BF16)],
        flops=2 * blocks * tiles * size * size * width,
    )(tile_cols, place, pair, far, adj_tiles, degrees.reshape(1, -1), w_self, w_neigh)

    packed = lax.all_to_all(packed, "feat", 0, 0, tiled=True)
    near_count = lax.axis_size("near")
    depth = feat_count * 2 * width
    pieces = (width // 2 + 1, 2, rows_own)
    share = call(
        share_kernel,
        jax.ShapeDtypeStruct((2 * depth + 2 * rows_own, rows_own), BF16),
        [VMEM] * 2,
    )(packed, cotangent)
    pair = lax.all_gather(share, "c")
    hidden, grads = call(
        layer_kernel,
        (
            jax.ShapeDtypeStruct((rows_own, hidden_units), BF16),
            jax.ShapeDtypeStruct((near_count, feat_count, *pieces), BF16),
        ),
        [VMEM] * 4,
        flops=6 * rows_own * depth * hidden_units,
    )(packed, pair, place, hidden_bias.reshape(1, -1))

    grads = lax.all_to_all(grads.reshape(near_count * feat_count, *pieces), ("near", "feat"), 0, 0, tiled=True)
    grads = call(sum_kernel, jax.ShapeDtypeStruct((chip_count, *pieces), BF16), [VMEM])(grads)
    grads = lax.all_to_all(grads, CHIPS, 0, 0, tiled=True)
    grads = call(total_kernel, jax.ShapeDtypeStruct((2 * width + 8, rows_own), F32), [VMEM])(grads)
    pair = lax.all_gather(grads, "c")
    hidden, grad_self, grad_neigh, grad_bias = call(
        output_kernel,
        (
            jax.ShapeDtypeStruct((rows_own, hidden_units), BF16),
            jax.ShapeDtypeStruct((width, hidden_units), F32),
            jax.ShapeDtypeStruct((width, hidden_units), F32),
            jax.ShapeDtypeStruct((1, hidden_units), F32),
        ),
        [VMEM] * 2,
    )(pair, hidden)
    return (hidden, grad_self, grad_neigh, grad_bias.reshape(hidden_units))


def solution(mesh):
    sizes = {"x": 4, "z": 4, "near": 2, "c": 2, "feat": 8}
    grid = Mesh(mesh.devices.reshape(tuple(sizes.values())), tuple(sizes))
    return jax.shard_map(
        shards,
        mesh=grid,
        in_specs=(
            P(VERTEX, "feat"),
            P(VERTEX, None, None, None),
            P(VERTEX, None),
            P(VERTEX),
            P("feat", None),
            P("feat", None),
            P(),
            P((*VERTEX, "feat"), None),
        ),
        out_specs=(P((*VERTEX, "feat"), None), P("feat", None), P("feat", None), P()),
        check_vma=False,
    )
```

```python
import functools

import jax
import jax.numpy as jnp
from jax import lax
from jax.experimental import pallas as pl
from jax.experimental.pallas import tpu as pltpu
from jax.sharding import Mesh, PartitionSpec as P

F32 = jnp.float32
BF16 = jnp.bfloat16
CHIPS = ("x", "z", "near")
VERTEX = ("x", "z", "near", "c")
NT = (((1,), (1,)), ((), ()))
TN = (((0,), (0,)), ((), ()))
VMEM = pl.BlockSpec(memory_space=pltpu.VMEM)
SMEM = pl.BlockSpec(memory_space=pltpu.SMEM)


def call(kernel, out_shape, in_specs, scratch_shapes=(), flops=0, out_specs=None):
    if out_specs is None:
        out_specs = [VMEM] * len(out_shape) if isinstance(out_shape, tuple) else VMEM
    return pl.pallas_call(
        kernel,
        out_shape=out_shape,
        in_specs=in_specs,
        out_specs=out_specs,
        scratch_shapes=list(scratch_shapes),
        compiler_params=pltpu.CompilerParams(vmem_limit_bytes=32 * 1024 * 1024),
        cost_estimate=pl.CostEstimate(flops=flops, bytes_accessed=2000000, transcendentals=0),
    )


def place_kernel(blocks, where_ref, place_ref):
    place_ref[...] = where_ref[...] * blocks


def aggregate_kernel(total_blocks, cols_ref, place_ref, pair_ref, far_ref, adj_ref, deg_ref, ws_ref, wn_ref, out_ref, feats):
    blocks, tiles, _, size = adj_ref.shape
    width = far_ref.shape[0]
    half = ws_ref.shape[1] // 2
    for b in range(blocks):
        feats[b] = pair_ref[0, :, b * size : (b + 1) * size]
        feats[blocks + b] = pair_ref[1, :, b * size : (b + 1) * size]
        feats[2 * blocks + b] = far_ref[:, b * size : (b + 1) * size]
    first = place_ref[0, 0]
    turn = place_ref[1, 0]
    own = place_ref[2, 0]
    weights_here = [jnp.where(own == 0, ref[:, :half], ref[:, half:]) for ref in (ws_ref, wn_ref)]

    def spot(col):
        col = col - first + blocks
        col = jnp.where(col < 0, col + total_blocks, col)
        col = jnp.where(col >= total_blocks, col - total_blocks, col) + turn
        return jnp.where(col >= 3 * blocks, col - 3 * blocks, col)

    for r in range(blocks):
        picked = jnp.concatenate([feats[spot(cols_ref[r, k])] for k in range(tiles)], axis=1)
        weights = jnp.concatenate([adj_ref[r, k] for k in range(tiles)], axis=1)
        total = lax.dot_general(picked, weights, NT, preferred_element_type=F32)
        degree = deg_ref[:, r * size : (r + 1) * size].astype(F32)
        out_ref[r, :width] = feats[own + r]
        out_ref[r, width : 2 * width] = (total / degree).astype(BF16)
        for i, part in enumerate(weights_here):
            out_ref[r, (2 + i) * width : (3 + i) * width] = part


def share_kernel(packed_ref, cot_ref, share_ref):
    feat_count, depth, rows = packed_ref.shape
    depth = feat_count * depth // 2
    share_ref[:depth] = packed_ref[:, : depth // feat_count].reshape(depth, rows)
    share_ref[depth : 2 * depth] = packed_ref[:, depth // feat_count :].reshape(depth, rows)
    for h in range(2):
        share_ref[2 * depth + h * rows : 2 * depth + (h + 1) * rows] = cot_ref[:, h * rows : (h + 1) * rows]


def layer_kernel(packed_ref, pair_ref, place_ref, bias_ref, hidden_ref, grads_ref):
    _, feat_count, pairs, _, half = grads_ref.shape
    pairs -= 1
    rows = packed_ref.shape[2]
    depth = feat_count * 4 * pairs
    cots = 2 * depth
    core = place_ref[2:3]
    inputs = packed_ref[:, : 4 * pairs].reshape(depth, rows)
    weights = packed_ref[:, 4 * pairs :].reshape(depth, half)
    units = jnp.concatenate([pair_ref[h, depth:cots] for h in range(2)], axis=1)
    preact = lax.dot_general(inputs, units, TN, preferred_element_type=F32) + bias_ref[...]
    hidden_ref[...] = jnp.maximum(preact, 0.0).astype(BF16)
    bias = jnp.where(core == 0, bias_ref[:, :half], bias_ref[:, half:])
    core = jnp.broadcast_to(core, (rows, half))
    inputs = jnp.concatenate([pair_ref[c, :depth] for c in range(2)], axis=1)
    preact = lax.dot_general(inputs, weights, TN, preferred_element_type=F32) + bias
    grad_pre = []
    for c in range(2):
        cot = jnp.where(
            core == 0,
            pair_ref[c, cots : cots + rows].astype(F32),
            pair_ref[c, cots + rows :].astype(F32),
        )
        grad_pre.append(jnp.where(preact[c * rows : (c + 1) * rows] > 0, cot, 0.0).astype(BF16))
    grad_pre = jnp.concatenate(grad_pre, axis=0)
    grads = jnp.dot(inputs, grad_pre, preferred_element_type=F32)
    ones = jnp.ones((8, 2 * rows), BF16)
    bias = jnp.dot(ones, grad_pre, preferred_element_type=F32)[:1]
    bias = jnp.concatenate([bias, jnp.zeros_like(bias)], axis=0).astype(BF16)
    grads = grads.reshape(feat_count, 2, pairs, 2, half).astype(BF16)
    for near in range(2):
        grads_ref[near, :, :pairs] = grads[:, near]
        for f in range(feat_count):
            grads_ref[near, f, pairs] = bias


def sum_kernel(rows_ref, out_ref):
    total = rows_ref[0].astype(F32)
    for i in range(1, rows_ref.shape[0]):
        total += rows_ref[i].astype(F32)
    total = total.astype(out_ref.dtype)
    for i in range(out_ref.shape[0]):
        out_ref[i] = total


def total_kernel(rows_ref, out_ref):
    pairs = rows_ref.shape[1] - 1
    for near in range(2):
        total = rows_ref[near].astype(F32)
        for i in range(near + 2, rows_ref.shape[0], 2):
            total += rows_ref[i].astype(F32)
        for i in range(pairs):
            first = 2 * (near * pairs + i)
            out_ref[first : first + 2] = total[i]
        if near == 0:
            out_ref[4 * pairs :] = jnp.zeros((out_ref.shape[0] - 4 * pairs, out_ref.shape[1]), F32)
            out_ref[4 * pairs : 4 * pairs + 2] = total[pairs]


def output_kernel(pair_ref, layer_ref, hidden_ref, self_ref, neigh_ref, bias_ref):
    width = self_ref.shape[0]
    half = pair_ref.shape[2]
    hidden_ref[...] = layer_ref[...]
    for h in range(2):
        lanes = slice(h * half, (h + 1) * half)
        self_ref[:, lanes] = pair_ref[h, :width]
        neigh_ref[:, lanes] = pair_ref[h, width : 2 * width]
        bias_ref[:, lanes] = pair_ref[h, 2 * width : 2 * width + 1]


def shards(node_feats, adj_tiles, tile_cols, degrees, w_self, w_neigh, hidden_bias, cotangent):
    node_count, width = node_feats.shape
    blocks, tiles, size, _ = adj_tiles.shape
    vertex_count = lax.axis_size(VERTEX)
    feat_count = lax.axis_size("feat")
    chip_count = vertex_count // 2
    rows_own = node_count // feat_count
    hidden_units = w_self.shape[1]

    feats = node_feats.T
    away = [(v, (v - 1 if v % 2 == 0 else v + 1) % vertex_count) for v in range(vertex_count)]
    far = lax.ppermute(feats, VERTEX, away)
    pair = lax.all_gather(feats, "c")
    vertex_idx = lax.axis_index(VERTEX)
    core = lax.axis_index("c")
    where = jnp.stack([vertex_idx, 2 * (1 - core), core]).astype(jnp.int32)
    place = call(
        functools.partial(place_kernel, blocks),
        jax.ShapeDtypeStruct((3, size), jnp.int32),
        [VMEM],
        flops=5 * 10**9,
    )(jnp.broadcast_to(where[:, None], (3, size)))
    packed = call(
        functools.partial(aggregate_kernel, blocks * vertex_count),
        jax.ShapeDtypeStruct((feat_count, 4 * width, rows_own), BF16),
        [SMEM] * 2 + [VMEM] * 6,
        [pltpu.VMEM((3 * blocks, width, size), BF16)],
        flops=2 * blocks * tiles * size * size * width,
    )(tile_cols, place, pair, far, adj_tiles, degrees.reshape(1, -1), w_self, w_neigh)

    packed = lax.all_to_all(packed, "feat", 0, 0, tiled=True)
    near_count = lax.axis_size("near")
    depth = feat_count * 2 * width
    pieces = (width // 2 + 1, 2, rows_own)
    share = call(
        share_kernel,
        jax.ShapeDtypeStruct((2 * depth + 2 * rows_own, rows_own), BF16),
        [VMEM] * 2,
    )(packed, cotangent)
    pair = lax.all_gather(share, "c")
    hidden, grads = call(
        layer_kernel,
        (
            jax.ShapeDtypeStruct((rows_own, hidden_units), BF16),
            jax.ShapeDtypeStruct((near_count, feat_count, *pieces), BF16),
        ),
        [VMEM] * 4,
        flops=6 * rows_own * depth * hidden_units,
    )(packed, pair, place, hidden_bias.reshape(1, -1))

    grads = lax.all_to_all(grads.reshape(near_count * feat_count, *pieces), ("near", "feat"), 0, 0, tiled=True)
    grads = call(sum_kernel, jax.ShapeDtypeStruct((chip_count, *pieces), BF16), [VMEM])(grads)
    grads = lax.all_to_all(grads, CHIPS, 0, 0, tiled=True)
    grads = call(total_kernel, jax.ShapeDtypeStruct((2 * width + 8, rows_own), F32), [VMEM])(grads)
    pair = lax.all_gather(grads, "c")
    hidden, grad_self, grad_neigh, grad_bias = call(
        output_kernel,
        (
            jax.ShapeDtypeStruct((rows_own, hidden_units), BF16),
            jax.ShapeDtypeStruct((width, hidden_units), F32),
            jax.ShapeDtypeStruct((width, hidden_units), F32),
            jax.ShapeDtypeStruct((1, hidden_units), F32),
        ),
        [VMEM] * 2,
    )(pair, hidden)
    return (hidden, grad_self, grad_neigh, grad_bias.reshape(hidden_units))


def solution(mesh):
    sizes = {"x": 4, "z": 4, "near": 2, "c": 2, "feat": 8}
    grid = Mesh(mesh.devices.reshape(tuple(sizes.values())), tuple(sizes))
    return jax.shard_map(
        shards,
        mesh=grid,
        in_specs=(
            P(VERTEX, "feat"),
            P(VERTEX, None, None, None),
            P(VERTEX, None),
            P(VERTEX),
            P("feat", None),
            P("feat", None),
            P(),
            P((*VERTEX, "feat"), None),
        ),
        out_specs=(P((*VERTEX, "feat"), None), P("feat", None), P("feat", None), P()),
        check_vma=False,
    )
```

```python
import functools

import jax
import jax.numpy as jnp
from jax import lax
from jax.experimental import pallas as pl
from jax.experimental.pallas import tpu as pltpu
from jax.sharding import Mesh, PartitionSpec as P

F32 = jnp.float32
BF16 = jnp.bfloat16
CHIPS = ("x", "z", "near")
VERTEX = ("x", "z", "near", "c")
NT = (((1,), (1,)), ((), ()))
TN = (((0,), (0,)), ((), ()))
VMEM = pl.BlockSpec(memory_space=pltpu.VMEM)
SMEM = pl.BlockSpec(memory_space=pltpu.SMEM)


def call(kernel, out_shape, in_specs, scratch_shapes=(), flops=0, out_specs=None):
    if out_specs is None:
        out_specs = [VMEM] * len(out_shape) if isinstance(out_shape, tuple) else VMEM
    return pl.pallas_call(
        kernel,
        out_shape=out_shape,
        in_specs=in_specs,
        out_specs=out_specs,
        scratch_shapes=list(scratch_shapes),
        compiler_params=pltpu.CompilerParams(vmem_limit_bytes=32 * 1024 * 1024),
        cost_estimate=pl.CostEstimate(flops=flops, bytes_accessed=2000000, transcendentals=0),
    )


def place_kernel(blocks, where_ref, place_ref):
    place_ref[...] = where_ref[...] * blocks


def aggregate_kernel(total_blocks, cols_ref, place_ref, pair_ref, far_ref, adj_ref, deg_ref, ws_ref, wn_ref, out_ref, feats):
    blocks, tiles, _, size = adj_ref.shape
    width = far_ref.shape[0]
    half = ws_ref.shape[1] // 2
    for b in range(blocks):
        feats[b] = pair_ref[0, :, b * size : (b + 1) * size]
        feats[blocks + b] = pair_ref[1, :, b * size : (b + 1) * size]
        feats[2 * blocks + b] = far_ref[:, b * size : (b + 1) * size]
    first = place_ref[0, 0]
    turn = place_ref[1, 0]
    own = place_ref[2, 0]
    weights_here = [jnp.where(own == 0, ref[:, :half], ref[:, half:]) for ref in (ws_ref, wn_ref)]

    def spot(col):
        col = col - first + blocks
        col = jnp.where(col < 0, col + total_blocks, col)
        col = jnp.where(col >= total_blocks, col - total_blocks, col) + turn
        return jnp.where(col >= 3 * blocks, col - 3 * blocks, col)

    for r in range(blocks):
        picked = jnp.concatenate([feats[spot(cols_ref[r, k])] for k in range(tiles)], axis=1)
        weights = jnp.concatenate([adj_ref[r, k] for k in range(tiles)], axis=1)
        total = lax.dot_general(picked, weights, NT, preferred_element_type=F32)
        degree = deg_ref[:, r * size : (r + 1) * size].astype(F32)
        out_ref[r, :width] = feats[own + r]
        out_ref[r, width : 2 * width] = (total / degree).astype(BF16)
        for i, part in enumerate(weights_here):
            out_ref[r, (2 + i) * width : (3 + i) * width] = part


def share_kernel(packed_ref, cot_ref, share_ref):
    feat_count, depth, rows = packed_ref.shape
    depth = feat_count * depth // 2
    share_ref[:depth] = packed_ref[:, : depth // feat_count].reshape(depth, rows)
    share_ref[depth : 2 * depth] = packed_ref[:, depth // feat_count :].reshape(depth, rows)
    for h in range(2):
        share_ref[2 * depth + h * rows : 2 * depth + (h + 1) * rows] = cot_ref[:, h * rows : (h + 1) * rows]


def layer_kernel(packed_ref, pair_ref, place_ref, bias_ref, hidden_ref, grads_ref):
    _, feat_count, pairs, _, half = grads_ref.shape
    pairs -= 1
    rows = packed_ref.shape[2]
    depth = feat_count * 4 * pairs
    cots = 2 * depth
    core = place_ref[2:3]
    inputs = packed_ref[:, : 4 * pairs].reshape(depth, rows)
    weights = packed_ref[:, 4 * pairs :].reshape(depth, half)
    units = jnp.concatenate([pair_ref[h, depth:cots] for h in range(2)], axis=1)
    preact = lax.dot_general(inputs, units, TN, preferred_element_type=F32) + bias_ref[...]
    hidden_ref[...] = jnp.maximum(preact, 0.0).astype(BF16)
    bias = jnp.where(core == 0, bias_ref[:, :half], bias_ref[:, half:])
    core = jnp.broadcast_to(core, (rows, half))
    inputs = jnp.concatenate([pair_ref[c, :depth] for c in range(2)], axis=1)
    preact = lax.dot_general(inputs, weights, TN, preferred_element_type=F32) + bias
    grad_pre = []
    for c in range(2):
        cot = jnp.where(
            core == 0,
            pair_ref[c, cots : cots + rows].astype(F32),
            pair_ref[c, cots + rows :].astype(F32),
        )
        grad_pre.append(jnp.where(preact[c * rows : (c + 1) * rows] > 0, cot, 0.0).astype(BF16))
    grad_pre = jnp.concatenate(grad_pre, axis=0)
    grads = jnp.dot(inputs, grad_pre, preferred_element_type=F32)
    ones = jnp.ones((8, 2 * rows), BF16)
    bias = jnp.dot(ones, grad_pre, preferred_element_type=F32)[:1]
    bias = jnp.concatenate([bias, jnp.zeros_like(bias)], axis=0).astype(BF16)
    for f in range(feat_count):
        for near in range(2):
            for i in range(pairs):
                first = (f * 2 + near) * 2 * pairs + 2 * i
                grads_ref[near, f, i] = grads[first : first + 2].astype(BF16)
            grads_ref[near, f, pairs] = bias


def sum_kernel(rows_ref, out_ref):
    total = rows_ref[0].astype(F32)
    for i in range(1, rows_ref.shape[0]):
        total += rows_ref[i].astype(F32)
    total = total.astype(out_ref.dtype)
    for i in range(out_ref.shape[0]):
        out_ref[i] = total


def total_kernel(rows_ref, out_ref):
    pairs = rows_ref.shape[1] - 1
    for near in range(2):
        total = rows_ref[near].astype(F32)
        for i in range(near + 2, rows_ref.shape[0], 2):
            total += rows_ref[i].astype(F32)
        for i in range(pairs):
            first = 2 * (near * pairs + i)
            out_ref[first : first + 2] = total[i]
        if near == 0:
            out_ref[4 * pairs :] = jnp.zeros((out_ref.shape[0] - 4 * pairs, out_ref.shape[1]), F32)
            out_ref[4 * pairs : 4 * pairs + 2] = total[pairs]


def output_kernel(pair_ref, layer_ref, hidden_ref, self_ref, neigh_ref, bias_ref):
    width = self_ref.shape[0]
    half = pair_ref.shape[2]
    hidden_ref[...] = layer_ref[...]
    for h in range(2):
        lanes = slice(h * half, (h + 1) * half)
        self_ref[:, lanes] = pair_ref[h, :width]
        neigh_ref[:, lanes] = pair_ref[h, width : 2 * width]
        bias_ref[:, lanes] = pair_ref[h, 2 * width : 2 * width + 1]


def shards(node_feats, adj_tiles, tile_cols, degrees, w_self, w_neigh, hidden_bias, cotangent):
    node_count, width = node_feats.shape
    blocks, tiles, size, _ = adj_tiles.shape
    vertex_count = lax.axis_size(VERTEX)
    feat_count = lax.axis_size("feat")
    chip_count = vertex_count // 2
    rows_own = node_count // feat_count
    hidden_units = w_self.shape[1]

    feats = node_feats.T
    away = [(v, (v - 1 if v % 2 == 0 else v + 1) % vertex_count) for v in range(vertex_count)]
    far = lax.ppermute(feats, VERTEX, away)
    pair = lax.all_gather(feats, "c")
    vertex_idx = lax.axis_index(VERTEX)
    core = lax.axis_index("c")
    where = jnp.stack([vertex_idx, 2 * (1 - core), core]).astype(jnp.int32)
    place = call(
        functools.partial(place_kernel, blocks),
        jax.ShapeDtypeStruct((3, size), jnp.int32),
        [VMEM],
        flops=5 * 10**8,
    )(jnp.broadcast_to(where[:, None], (3, size)))
    packed = call(
        functools.partial(aggregate_kernel, blocks * vertex_count),
        jax.ShapeDtypeStruct((feat_count, 4 * width, rows_own), BF16),
        [SMEM] * 2 + [VMEM] * 6,
        [pltpu.VMEM((3 * blocks, width, size), BF16)],
        flops=2 * blocks * tiles * size * size * width,
    )(tile_cols, place, pair, far, adj_tiles, degrees.reshape(1, -1), w_self, w_neigh)

    packed = lax.all_to_all(packed, "feat", 0, 0, tiled=True)
    near_count = lax.axis_size("near")
    depth = feat_count * 2 * width
    pieces = (width // 2 + 1, 2, rows_own)
    share = call(
        share_kernel,
        jax.ShapeDtypeStruct((2 * depth + 2 * rows_own, rows_own), BF16),
        [VMEM] * 2,
    )(packed, cotangent)
    pair = lax.all_gather(share, "c")
    hidden, grads = call(
        layer_kernel,
        (
            jax.ShapeDtypeStruct((rows_own, hidden_units), BF16),
            jax.ShapeDtypeStruct((near_count, feat_count, *pieces), BF16),
        ),
        [VMEM] * 4,
        flops=6 * rows_own * depth * hidden_units,
    )(packed, pair, place, hidden_bias.reshape(1, -1))

    grads = lax.all_to_all(grads.reshape(near_count * feat_count, *pieces), ("near", "feat"), 0, 0, tiled=True)
    grads = call(sum_kernel, jax.ShapeDtypeStruct((chip_count, *pieces), BF16), [VMEM])(grads)
    grads = lax.all_to_all(grads, CHIPS, 0, 0, tiled=True)
    grads = call(total_kernel, jax.ShapeDtypeStruct((2 * width + 8, rows_own), F32), [VMEM])(grads)
    pair = lax.all_gather(grads, "c")
    hidden, grad_self, grad_neigh, grad_bias = call(
        output_kernel,
        (
            jax.ShapeDtypeStruct((rows_own, hidden_units), BF16),
            jax.ShapeDtypeStruct((width, hidden_units), F32),
            jax.ShapeDtypeStruct((width, hidden_units), F32),
            jax.ShapeDtypeStruct((1, hidden_units), F32),
        ),
        [VMEM] * 2,
    )(pair, hidden)
    return (hidden, grad_self, grad_neigh, grad_bias.reshape(hidden_units))


def solution(mesh):
    sizes = {"x": 4, "z": 4, "near": 2, "c": 2, "feat": 8}
    grid = Mesh(mesh.devices.reshape(tuple(sizes.values())), tuple(sizes))
    return jax.shard_map(
        shards,
        mesh=grid,
        in_specs=(
            P(VERTEX, "feat"),
            P(VERTEX, None, None, None),
            P(VERTEX, None),
            P(VERTEX),
            P("feat", None),
            P("feat", None),
            P(),
            P((*VERTEX, "feat"), None),
        ),
        out_specs=(P((*VERTEX, "feat"), None), P("feat", None), P("feat", None), P()),
        check_vma=False,
    )
```
